32 devices in a mesh: dp: 16 (over z, y, x), tensor: 2 (over core).
Axes of the slice: x: 2, y: 2, z: 4, core: 2. Of those that a mesh axis runs over, the one named last changes fastest.
Arguments:
- queries: bfloat16 [16384, 3072], P('dp', 'tensor'), may hold values from -70 to 70
- keys: bfloat16 [16384, 3072], P('dp', 'tensor'), may hold values from -5 to 5
- values: bfloat16 [16384, 3072], P('dp', 'tensor'), may hold values from -6 to 6
- out_gradient: bfloat16 [16384, 5120], P(('dp', 'tensor')), may hold values from -6 to 6
- out_weight: bfloat16 [3072, 5120], P('tensor'), may hold values from -0.109375 to 0.109375
- segments: int32 [16, 8], replicated, may hold values from 0 to 7, as said below
- counts: int32 [16], replicated, may hold values from 1 to 4, as said below
Outputs:
- query_gradient: bfloat16 [16384, 3072], P('dp', 'tensor')
- key_gradient: bfloat16 [16384, 3072], P('dp', 'tensor')
- value_gradient: bfloat16 [16384, 3072], P('dp', 'tensor')
- weight_gradient: float32 [5120, 3072], P('dp', 'tensor')
The draws below stay inside these ranges and needn't reach their ends.
Inputs may be any that keep to these rules, and one draw needn't show every extreme that they name: `segments`: along each row ids never fall; each protein spans 1 to 4 consecutive blocks, and some protein spans exactly 4; the last counts[r] blocks of replica r are whole proteins. counts[r] equals counts[(r + 8) mod 16].
All inputs are finite; a program needn't handle non-finite values.
Results may differ from the reference program's by a relative error of at most 0.025.
Values may be sent and summed in bfloat16 or wider, within the bound.
A program may use at most 192 MiB of HBM per device.

```python
import jax
import jax.numpy as jnp
from jax import lax

D = 5120
HEADS = 24
HEAD_SIZE = 128
BLOCK = 128
BLOCKS = 8
MOVABLE = 4
INNER = 3072
REPLICAS = 16
REPLICA_ROWS = 1024
ROWS = 16384


def base_keys(key):
    raw = jnp.clip(jax.random.normal(jax.random.fold_in(key, 11), (ROWS, INNER), jnp.float32), -5.0, 5.0)
    return raw


def draw_keys(key, part):
    raw = base_keys(key)
    return raw.astype(jnp.bfloat16)


def draw_queries(key, part):
    raw = jnp.clip(jax.random.normal(jax.random.fold_in(key, 12), (ROWS, INNER), jnp.float32), -5.0, 5.0)
    return raw.astype(jnp.bfloat16)


def plan_tables(key):
    base = jax.random.fold_in(key, 21)
    pairs = REPLICAS // 2
    moves = jax.random.randint(jax.random.fold_in(base, 1), (pairs,), 1, MOVABLE + 1)
    moves = moves.at[1].set(1).at[0].set(MOVABLE)
    heavy_upper = jax.random.randint(jax.random.fold_in(base, 2), (pairs,), 0, 2)
    wanted = jax.random.randint(jax.random.fold_in(base, 3), (REPLICAS, BLOCKS), 0, 2)
    moved = jnp.concatenate([moves, moves])
    heavy = jnp.concatenate([1 - heavy_upper, heavy_upper])
    column = jnp.arange(BLOCKS)[None, :]
    boundary = BLOCKS - moved[:, None]
    in_tail = column >= boundary
    tail_start = jnp.where(heavy[:, None] == 1, column == boundary, True)
    head_start = (wanted == 1) | (column == 0)

    def advance(run, items):
        tail_here, tail_begin, head_begin = items
        begin = jnp.where(tail_here, tail_begin, head_begin | (run >= MOVABLE))
        return (jnp.where(begin, 1, run + 1), begin)
    final_run, begins = lax.scan(advance, jnp.zeros((REPLICAS,), jnp.int32), (in_tail.T, tail_start.T, head_start.T))
    protein_ids = jnp.cumsum(begins.T.astype(jnp.int32), axis=1) - 1
    return (protein_ids.astype(jnp.int32), moved.astype(jnp.int32))


def draw_segments(key, part):
    return plan_tables(key)[0]


def draw_counts(key, part):
    return plan_tables(key)[1]


def with_spikes(values, stream_key, source, target, shards_of, factor):
    owner, partner = [(jnp.arange(values.shape[axis_at]) // (values.shape[axis_at] // shards_of)).reshape([-1 if axis == axis_at else 1 for axis in range(values.ndim)]) for axis_at in (source, target)]
    chosen = jax.random.permutation(stream_key, shards_of)[partner]
    strong = (owner == chosen) | (owner == (partner + shards_of // 2) % shards_of)
    return jnp.where(strong, factor * values, values)


def block_scale(stream_key, dims, pieces, least, top_value):
    factor_of = 1.0
    for dim, parts in pieces:
        heights = jax.random.uniform(jax.random.fold_in(jax.random.fold_in(stream_key, 6), dim), (parts,), jnp.float32, least / len(pieces), top_value / len(pieces))
        factor_of = factor_of * jnp.repeat(jnp.exp(heights), dims[dim] // parts).reshape((-1,) + (1,) * (len(dims) - 1 - dim))
    return factor_of


def scatter_about(key, shape, spread, most, split=(), kind=jnp.bfloat16):
    factor_of = block_scale(key, shape, split, -0.22, 0.18) if split else 1.0
    drawn = jax.random.normal(key, shape, jnp.float32) * spread * factor_of
    return jnp.minimum(jnp.maximum(drawn, -most), most).astype(kind)


def gaussian_with(stream_key, dims, scale, reach, cuts, heavy, kind=jnp.bfloat16):
    entries = scale * jax.random.normal(stream_key, dims, jnp.float32)
    if cuts:
        entries = entries * block_scale(stream_key, dims, cuts, -0.22, 0.18)
    return jnp.clip(with_spikes(entries, jax.random.fold_in(stream_key, 3), *heavy), -reach, reach).astype(kind)


def setup_inputs(seed: int = 0) -> dict:
    key_list = jax.random.split(jax.random.key(seed), 8)
    return {
        "queries": draw_queries(jax.random.fold_in(key_list[7], 71), 0),
        "keys": draw_keys(jax.random.fold_in(key_list[7], 71), 0),
        "values": scatter_about(key_list[2], (ROWS, INNER), 1.0, 6.0, ((0, 16), (1, 2))),
        "out_gradient": gaussian_with(key_list[3], (ROWS, D), 1.0, 6.0, ((0, 32),), (0, 1, 32, 2.75)),
        "out_weight": scatter_about(key_list[4], (INNER, D), INNER ** -0.5, 0.109375, ((0, 2),)),
        "segments": draw_segments(jax.random.fold_in(key_list[7], 71), 0),
        "counts": draw_counts(jax.random.fold_in(key_list[7], 71), 0),
    }


masked_score = -1.0e30


def replica_backward(query, key_rows, value, gradient, seg_row):
    length = query.shape[0]
    scale = HEAD_SIZE ** -0.5
    protein = jnp.repeat(seg_row, BLOCK)
    matching = protein[:, None] == protein[None, :]
    query_heads = query.reshape(length, HEADS, HEAD_SIZE).astype(jnp.float32)
    key_heads = key_rows.reshape(length, HEADS, HEAD_SIZE).astype(jnp.float32)
    value_heads = value.reshape(length, HEADS, HEAD_SIZE).astype(jnp.float32)
    grad_heads = gradient.reshape(length, HEADS, HEAD_SIZE).astype(jnp.float32)
    scores = jnp.einsum("qhd,khd->hqk", query_heads, key_heads) * scale
    scores = jnp.where(matching[None], scores, masked_score)
    highest = jnp.max(scores, axis=2, keepdims=True)
    weights = jnp.exp(scores - highest)
    chances = weights / jnp.sum(weights, axis=2, keepdims=True)
    chance_weights = lax.optimization_barrier(chances.astype(jnp.bfloat16)).astype(jnp.float32)
    head_output = jnp.einsum("hqk,khd->qhd", chance_weights, value_heads).astype(jnp.bfloat16)
    output_wide = lax.optimization_barrier(head_output).astype(jnp.float32)
    centering = jnp.sum(grad_heads * output_wide, axis=2)
    chance_gradient = jnp.einsum("qhd,khd->hqk", grad_heads, value_heads)
    score_gradient = chances * (chance_gradient - jnp.transpose(centering)[:, :, None])
    score_gradient = lax.optimization_barrier(score_gradient.astype(jnp.bfloat16)).astype(jnp.float32)
    query_local = (jnp.einsum("hqk,khd->qhd", score_gradient, key_heads) * scale).astype(jnp.bfloat16)
    key_local = (jnp.einsum("hqk,qhd->khd", score_gradient, query_heads) * scale).astype(jnp.bfloat16)
    value_local = jnp.einsum("hqk,qhd->khd", chance_weights, grad_heads).astype(jnp.bfloat16)
    return (query_local.reshape(length, INNER), key_local.reshape(length, INNER),
            value_local.reshape(length, INNER), head_output.reshape(length, INNER))


def by_replica(items):
    return replica_backward(items[0], items[1], items[2], items[3], items[4])


def reference(queries, keys, values, out_gradient, out_weight, segments, counts):
    head_gradient = lax.dot_general(out_gradient, out_weight, (((1,), (1,)), ((), ())),
                                    preferred_element_type=jnp.float32).astype(jnp.bfloat16)

    def shaped(array):
        return array.reshape(REPLICAS, REPLICA_ROWS, INNER)

    query_local, key_local, value_local, head_output = lax.map(
        by_replica, (shaped(queries), shaped(keys), shaped(values), shaped(head_gradient), segments))
    output_flat = head_output.reshape(ROWS, INNER)
    weight_gradient = lax.dot_general(out_gradient, output_flat, (((0,), (0,)), ((), ())),
                                      preferred_element_type=jnp.float32) / REPLICAS
    moved = jnp.arange(BLOCKS, dtype=jnp.int32)[None, :] >= (BLOCKS - counts)[:, None]

    def settle(array):
        blocked = array.reshape(REPLICAS, BLOCKS, BLOCK, INNER)
        partner = jnp.roll(blocked, REPLICAS // 2, axis=0)
        return jnp.where(moved[:, :, None, None], partner, blocked).reshape(ROWS, INNER)

    return settle(query_local), settle(key_local), settle(value_local), weight_gradient
```

```python
import functools
import math

import jax
import jax.numpy as jnp
from jax import lax
from jax.experimental import pallas as pl
from jax.experimental.pallas import tpu as pltpu
from jax.sharding import PartitionSpec as P

HEAD_SIZE = 128
BLOCK = 128

masked_score = -1e30


def contract(a, b, dims):
    return lax.dot_general(a, b, (dims, ((), ())), preferred_element_type=jnp.float32)


def attend_kernel(
    window, starts, same, q_ref, k_ref, v_ref, g_ref, lead_ref, trail_ref, out_ref, key_sum, value_sum
):
    length = q_ref.shape[0]
    blocks = length // BLOCK
    half = lead_ref.shape[1]
    scale = HEAD_SIZE ** (-0.5)
    exponent = scale * math.log2(math.e)
    key_sum[...] = jnp.zeros_like(key_sum)
    value_sum[...] = jnp.zeros_like(value_sum)
    for index in range(blocks):
        rows = slice(index * BLOCK, (index + 1) * BLOCK)
        span = pl.ds(pl.multiple_of(starts[index] * BLOCK, BLOCK), window * BLOCK)
        query, grad = q_ref[rows, :], g_ref[rows, :]
        keys, values = k_ref[span, :], v_ref[span, :]
        raw = contract(keys, query, ((1,), (1,))) * exponent
        scores = jnp.concatenate(
            [
                raw[tile * BLOCK : (tile + 1) * BLOCK]
                + jnp.where(same[index * window + tile] == 1, 0.0, masked_score)
                for tile in range(window)
            ],
            axis=0,
        )
        weights = jnp.exp2(scores - jnp.max(scores, axis=0, keepdims=True))
        chances = weights * (1.0 / jnp.sum(weights, axis=0, keepdims=True))
        chance_weights = chances.astype(jnp.bfloat16)
        output = contract(values, chance_weights, ((0,), (0,))).astype(jnp.bfloat16)
        grad_turned = grad.astype(jnp.float32).T
        centering = jnp.sum(grad_turned * output.astype(jnp.float32), axis=0, keepdims=True)
        chance_gradient = contract(values, grad, ((1,), (1,)))
        slopes = (chances * (chance_gradient - centering)).astype(jnp.bfloat16)
        query_turned = contract(keys, slopes, ((0,), (0,))) * scale
        out_ref[rows, :] = output.astype(jnp.float32).T.astype(jnp.bfloat16)
        query_local = query_turned.T.astype(jnp.bfloat16)
        if index * BLOCK < half:
            lead_ref[0, rows, :] = query_local
        else:
            trail_ref[0, index * BLOCK - half : (index + 1) * BLOCK - half, :] = query_local
        key_sum[span, :] += contract(slopes, query, ((1,), (0,)))
        value_sum[span, :] += contract(chance_weights, grad, ((1,), (0,)))
    key_local = (key_sum[...] * scale).astype(jnp.bfloat16)
    value_local = value_sum[...].astype(jnp.bfloat16)
    lead_ref[1] = key_local[:half]
    trail_ref[1] = key_local[half:]
    lead_ref[2] = value_local[:half]
    trail_ref[2] = value_local[half:]


def attend(query, key_rows, value, gradient, starts, same, first, heads, window, trailing):
    length = query.shape[0]
    columns = heads * HEAD_SIZE
    lead = length - trailing
    whole = pl.BlockSpec((length, HEAD_SIZE), lambda head, *_: (0, head + first))
    own = pl.BlockSpec((length, HEAD_SIZE), lambda head, *_: (0, head))
    return pl.pallas_call(
        functools.partial(attend_kernel, window),
        out_shape=(
            jax.ShapeDtypeStruct((3, lead, columns), jnp.bfloat16),
            jax.ShapeDtypeStruct((3, trailing, columns), jnp.bfloat16),
            jax.ShapeDtypeStruct((length, columns), jnp.bfloat16),
        ),
        grid_spec=pltpu.PrefetchScalarGridSpec(
            num_scalar_prefetch=2,
            grid=(heads,),
            in_specs=[whole, whole, whole, own],
            out_specs=(
                pl.BlockSpec((3, lead, HEAD_SIZE), lambda head, *_: (0, 0, head)),
                pl.BlockSpec((3, trailing, HEAD_SIZE), lambda head, *_: (0, 0, head)),
                own,
            ),
            scratch_shapes=[
                pltpu.VMEM((length, HEAD_SIZE), jnp.float32),
                pltpu.VMEM((length, HEAD_SIZE), jnp.float32),
            ],
        ),
        compiler_params=pltpu.CompilerParams(vmem_limit_bytes=32 * 1024 * 1024),
        cost_estimate=pl.CostEstimate(
            flops=10 * length * window * BLOCK * columns,
            bytes_accessed=16 * length * columns,
            transcendentals=length * window * BLOCK * heads,
        ),
    )(starts, same, query, key_rows, value, gradient)


def shards(queries, keys, values, out_gradient, out_weight, segments, counts):
    full_gradient = lax.all_gather(out_gradient, "tensor", axis=0, tiled=True)
    replicas = lax.axis_size("dp")
    halfway = replicas // 2
    position = lax.axis_index("dp")
    blocks = segments.shape[1]
    window = blocks // 2
    trailing = window * BLOCK
    heads = queries.shape[1] // HEAD_SIZE
    groups = max(count for count in (1, 2, 3) if heads % count == 0)
    each = heads // groups
    moving = lax.dynamic_index_in_dim(counts, position, 0, keepdims=False)
    ids = lax.dynamic_index_in_dim(segments, position, 0, keepdims=False)
    firsts = jnp.argmax(ids[:, None] == ids[None, :], axis=1).astype(jnp.int32)
    starts = jnp.minimum(firsts, blocks - window)
    near = jnp.take(ids, starts[:, None] + jnp.arange(window, dtype=jnp.int32)[None, :])
    same = (near == ids[:, None]).astype(jnp.int32).reshape(-1)
    block_moved = jnp.arange(blocks, dtype=jnp.int32) >= blocks - moving
    row_moved = jnp.repeat(block_moved, BLOCK)[-trailing:, None]
    pairs = [(i, (i + halfway) % replicas) for i in range(replicas)]

    leads, trails, weight_parts = [], [], []
    for group in range(groups):
        width = each * HEAD_SIZE
        head_gradient = contract(
            full_gradient, out_weight[group * width : (group + 1) * width], ((1,), (1,))
        ).astype(jnp.bfloat16)
        lead, trail, head_output = attend(
            queries, keys, values, head_gradient, starts, same, group * each, each, window, trailing
        )
        arrived = lax.ppermute(trail, "dp", pairs)
        leads.append(lead)
        trails.append((trail, arrived))
        term = (contract(full_gradient, head_output, ((0,), (0,))) / replicas).astype(jnp.bfloat16)
        weight_parts.append(lax.psum_scatter(term, "dp", scatter_dimension=0, tiled=True))

    def settled(which):
        upper = jnp.concatenate([lead[which] for lead in leads], axis=1)
        lower = jnp.concatenate(
            [jnp.where(row_moved, arrived[which], trail[which]) for trail, arrived in trails], axis=1
        )
        return jnp.concatenate([upper, lower], axis=0)

    weight_gradient = jnp.concatenate(weight_parts, axis=1).astype(jnp.float32)
    return (settled(0), settled(1), settled(2), weight_gradient)


def solution(mesh):
    in_specs = (
        P("dp", "tensor"),
        P("dp", "tensor"),
        P("dp", "tensor"),
        P(("dp", "tensor"), None),
        P("tensor", None),
        P(),
        P(),
    )
    out_specs = (P("dp", "tensor"), P("dp", "tensor"), P("dp", "tensor"), P("dp", "tensor"))
    return jax.shard_map(shards, mesh=mesh, in_specs=in_specs, out_specs=out_specs, check_vma=False)
```

```python
import functools
import math

import jax
import jax.numpy as jnp
from jax import lax
from jax.experimental import pallas as pl
from jax.experimental.pallas import tpu as pltpu
from jax.sharding import PartitionSpec as P

HEAD_SIZE = 128
BLOCK = 128

masked_score = -1e30


def contract(a, b, dims):
    return lax.dot_general(a, b, (dims, ((), ())), preferred_element_type=jnp.float32)


def attend_kernel(
    window, starts, same, q_ref, k_ref, v_ref, g_ref, lead_ref, trail_ref, out_ref, key_sum, value_sum
):
    length = q_ref.shape[0]
    blocks = length // BLOCK
    half = lead_ref.shape[1]
    scale = HEAD_SIZE ** (-0.5)
    exponent = scale * math.log2(math.e)
    key_sum[...] = jnp.zeros_like(key_sum)
    value_sum[...] = jnp.zeros_like(value_sum)
    for index in range(blocks):
        rows = slice(index * BLOCK, (index + 1) * BLOCK)
        span = pl.ds(pl.multiple_of(starts[index] * BLOCK, BLOCK), window * BLOCK)
        query, grad = q_ref[rows, :], g_ref[rows, :]
        keys, values = k_ref[span, :], v_ref[span, :]
        raw = contract(keys, query, ((1,), (1,))) * exponent
        scores = jnp.concatenate(
            [
                raw[tile * BLOCK : (tile + 1) * BLOCK]
                + jnp.where(same[index * window + tile] == 1, 0.0, masked_score)
                for tile in range(window)
            ],
            axis=0,
        )
        weights = jnp.exp2(scores - jnp.max(scores, axis=0, keepdims=True))
        chances = weights * (1.0 / jnp.sum(weights, axis=0, keepdims=True))
        chance_weights = chances.astype(jnp.bfloat16)
        output = contract(values, chance_weights, ((0,), (0,))).astype(jnp.bfloat16)
        grad_turned = grad.astype(jnp.float32).T
        centering = jnp.sum(grad_turned * output.astype(jnp.float32), axis=0, keepdims=True)
        chance_gradient = contract(values, grad, ((1,), (1,)))
        slopes = (chances * (chance_gradient - centering)).astype(jnp.bfloat16)
        query_turned = contract(keys, slopes, ((0,), (0,))) * scale
        out_ref[rows, :] = output.astype(jnp.float32).T.astype(jnp.bfloat16)
        query_local = query_turned.T.astype(jnp.bfloat16)
        if index * BLOCK < half:
            lead_ref[0, rows, :] = query_local
        else:
            trail_ref[0, index * BLOCK - half : (index + 1) * BLOCK - half, :] = query_local
        key_sum[span, :] += contract(slopes, query, ((1,), (0,)))
        value_sum[span, :] += contract(chance_weights, grad, ((1,), (0,)))
    key_local = (key_sum[...] * scale).astype(jnp.bfloat16)
    value_local = value_sum[...].astype(jnp.bfloat16)
    lead_ref[1] = key_local[:half]
    trail_ref[1] = key_local[half:]
    lead_ref[2] = value_local[:half]
    trail_ref[2] = value_local[half:]


def attend(query, key_rows, value, gradient, starts, same, first, heads, window, trailing):
    length = query.shape[0]
    columns = heads * HEAD_SIZE
    lead = length - trailing
    whole = pl.BlockSpec((length, HEAD_SIZE), lambda head, *_: (0, head + first))
    own = pl.BlockSpec((length, HEAD_SIZE), lambda head, *_: (0, head))
    return pl.pallas_call(
        functools.partial(attend_kernel, window),
        out_shape=(
            jax.ShapeDtypeStruct((3, lead, columns), jnp.bfloat16),
            jax.ShapeDtypeStruct((3, trailing, columns), jnp.bfloat16),
            jax.ShapeDtypeStruct((length, columns), jnp.bfloat16),
        ),
        grid_spec=pltpu.PrefetchScalarGridSpec(
            num_scalar_prefetch=2,
            grid=(heads,),
            in_specs=[whole, whole, whole, own],
            out_specs=(
                pl.BlockSpec((3, lead, HEAD_SIZE), lambda head, *_: (0, 0, head)),
                pl.BlockSpec((3, trailing, HEAD_SIZE), lambda head, *_: (0, 0, head)),
                own,
            ),
            scratch_shapes=[
                pltpu.VMEM((length, HEAD_SIZE), jnp.float32),
                pltpu.VMEM((length, HEAD_SIZE), jnp.float32),
            ],
        ),
        compiler_params=pltpu.CompilerParams(vmem_limit_bytes=32 * 1024 * 1024),
        cost_estimate=pl.CostEstimate(
            flops=10 * length * window * BLOCK * columns,
            bytes_accessed=16 * length * columns,
            transcendentals=length * window * BLOCK * heads,
        ),
    )(starts, same, query, key_rows, value, gradient)


def scattered(term, order):
    replicas = lax.axis_size("dp")
    position = lax.axis_index("dp")
    rows, columns = term.shape[0] // replicas, term.shape[1]
    remaining = list(reversed(range(replicas.bit_length() - 1)))
    for bit in order:
        place = remaining.index(bit)
        remaining.pop(place)
        below = len(remaining) - place
        halves = term.reshape(1 << place, 2, (1 << below) * rows, columns)
        mine = (position >> bit) & 1
        sent = lax.dynamic_index_in_dim(halves, 1 - mine, 1, keepdims=False)
        kept = lax.dynamic_index_in_dim(halves, mine, 1, keepdims=False)
        arrived = lax.ppermute(sent, "dp", [(i, i ^ 1 << bit) for i in range(replicas)])
        total = kept.astype(jnp.float32) + arrived.astype(jnp.float32)
        term = total.reshape(-1, columns)
        if remaining:
            term = term.astype(jnp.bfloat16)
    return term


def settle_kernel(blocks, moving, lead_ref, trail_ref, arrived_ref, *refs):
    outs = refs[-3:]
    half = lead_ref.shape[1]
    for which in range(3):
        outs[which][:half, :] = lead_ref[which]
        for block in range(trail_ref.shape[1] // BLOCK):
            rows = slice(block * BLOCK, (block + 1) * BLOCK)
            moved = half // BLOCK + block >= blocks - moving[0]

            @pl.when(moved)
            def _():
                outs[which][half + block * BLOCK : half + (block + 1) * BLOCK, :] = arrived_ref[which, rows]

            @pl.when(jnp.logical_not(moved))
            def _():
                outs[which][half + block * BLOCK : half + (block + 1) * BLOCK, :] = trail_ref[which, rows]


def settle(moving, lead, trail, arrived, first, heads, shape, earlier):
    step = lambda rows: pl.BlockSpec((3, rows, HEAD_SIZE), lambda head, *_: (0, 0, head))
    length = shape[0]
    return pl.pallas_call(
        functools.partial(settle_kernel, length // BLOCK),
        out_shape=(jax.ShapeDtypeStruct(shape, jnp.bfloat16),) * 3,
        grid_spec=pltpu.PrefetchScalarGridSpec(
            num_scalar_prefetch=1,
            grid=(heads,),
            in_specs=[step(lead.shape[1]), step(trail.shape[1]), step(trail.shape[1])]
            + [pl.BlockSpec(memory_space=pl.ANY)] * len(earlier),
            out_specs=(pl.BlockSpec((length, HEAD_SIZE), lambda head, *_: (0, head + first)),) * 3,
        ),
        input_output_aliases={4 + which: which for which in range(len(earlier))},
        compiler_params=pltpu.CompilerParams(vmem_limit_bytes=32 * 1024 * 1024),
        cost_estimate=pl.CostEstimate(
            flops=0, bytes_accessed=15 * length * heads * HEAD_SIZE, transcendentals=0
        ),
    )(moving.reshape(1), lead, trail, arrived, *earlier)


def shards(queries, keys, values, out_gradient, out_weight, segments, counts):
    full_gradient = lax.all_gather(out_gradient, "tensor", axis=0, tiled=True)
    replicas = lax.axis_size("dp")
    halfway = replicas // 2
    position = lax.axis_index("dp")
    blocks = segments.shape[1]
    window = blocks // 2
    trailing = window * BLOCK
    heads = queries.shape[1] // HEAD_SIZE
    groups = 2 if heads % 2 == 0 else min(heads, 3)
    each = heads // groups
    moving = lax.dynamic_index_in_dim(counts, position, 0, keepdims=False)
    ids = lax.dynamic_index_in_dim(segments, position, 0, keepdims=False)
    firsts = jnp.argmax(ids[:, None] == ids[None, :], axis=1).astype(jnp.int32)
    starts = jnp.minimum(firsts, blocks - window)
    near = jnp.take(ids, starts[:, None] + jnp.arange(window, dtype=jnp.int32)[None, :])
    same = (near == ids[:, None]).astype(jnp.int32).reshape(-1)
    pairs = [(i, (i + halfway) % replicas) for i in range(replicas)]
    upward = list(range(replicas.bit_length() - 1))
    orders = [upward, [1, 0] + upward[2:]]

    moves, weight_parts = [], []
    for group in range(groups):
        width = each * HEAD_SIZE
        head_gradient = contract(
            full_gradient, out_weight[group * width : (group + 1) * width], ((1,), (1,))
        ).astype(jnp.bfloat16)
        lead, trail, head_output = attend(
            queries, keys, values, head_gradient, starts, same, group * each, each, window, trailing
        )
        moves.append((lead, trail, lax.ppermute(trail, "dp", pairs)))
        term = (contract(full_gradient, head_output, ((0,), (0,))) / replicas).astype(jnp.bfloat16)
        weight_parts.append(scattered(term, orders[group % 2]))

    settled = ()
    for group, (lead, trail, arrived) in enumerate(moves):
        settled = settle(
            moving, lead, trail, arrived, group * each, each, queries.shape, settled
        )
    return (*settled, jnp.concatenate(weight_parts, axis=1))


def solution(mesh):
    in_specs = (
        P("dp", "tensor"),
        P("dp", "tensor"),
        P("dp", "tensor"),
        P(("dp", "tensor"), None),
        P("tensor", None),
        P(),
        P(),
    )
    out_specs = (P("dp", "tensor"), P("dp", "tensor"), P("dp", "tensor"), P("dp", "tensor"))
    return jax.shard_map(shards, mesh=mesh, in_specs=in_specs, out_specs=out_specs, check_vma=False)
```

```python
import functools
import math

import jax
import jax.numpy as jnp
from jax import lax
from jax.experimental import pallas as pl
from jax.experimental.pallas import tpu as pltpu
from jax.sharding import PartitionSpec as P

HEAD_SIZE = 128
BLOCK = 128

masked_score = -1e30


def contract(a, b, dims):
    return lax.dot_general(a, b, (dims, ((), ())), preferred_element_type=jnp.float32)


def attend_kernel(
    window, starts, same, q_ref, k_ref, v_ref, g_ref, lead_ref, trail_ref, out_ref, key_sum, value_sum
):
    length = q_ref.shape[0]
    blocks = length // BLOCK
    half = lead_ref.shape[1]
    scale = HEAD_SIZE ** (-0.5)
    exponent = scale * math.log2(math.e)
    key_sum[...] = jnp.zeros_like(key_sum)
    value_sum[...] = jnp.zeros_like(value_sum)
    for index in range(blocks):
        rows = slice(index * BLOCK, (index + 1) * BLOCK)
        span = pl.ds(pl.multiple_of(starts[index] * BLOCK, BLOCK), window * BLOCK)
        query, grad = q_ref[rows, :], g_ref[rows, :]
        keys, values = k_ref[span, :], v_ref[span, :]
        raw = contract(keys, query, ((1,), (1,))) * exponent
        scores = jnp.concatenate(
            [
                raw[tile * BLOCK : (tile + 1) * BLOCK]
                + jnp.where(same[index * window + tile] == 1, 0.0, masked_score)
                for tile in range(window)
            ],
            axis=0,
        )
        weights = jnp.exp2(scores - jnp.max(scores, axis=0, keepdims=True))
        chances = weights * (1.0 / jnp.sum(weights, axis=0, keepdims=True))
        chance_weights = chances.astype(jnp.bfloat16)
        output = contract(values, chance_weights, ((0,), (0,))).astype(jnp.bfloat16)
        grad_turned = grad.astype(jnp.float32).T
        centering = jnp.sum(grad_turned * output.astype(jnp.float32), axis=0, keepdims=True)
        chance_gradient = contract(values, grad, ((1,), (1,)))
        slopes = (chances * (chance_gradient - centering)).astype(jnp.bfloat16)
        query_turned = contract(keys, slopes, ((0,), (0,))) * scale
        out_ref[rows, :] = output.astype(jnp.float32).T.astype(jnp.bfloat16)
        query_local = query_turned.T.astype(jnp.bfloat16)
        if index * BLOCK < half:
            lead_ref[0, rows, :] = query_local
        else:
            trail_ref[0, index * BLOCK - half : (index + 1) * BLOCK - half, :] = query_local
        key_sum[span, :] += contract(slopes, query, ((1,), (0,)))
        value_sum[span, :] += contract(chance_weights, grad, ((1,), (0,)))
    key_local = (key_sum[...] * scale).astype(jnp.bfloat16)
    value_local = value_sum[...].astype(jnp.bfloat16)
    lead_ref[1] = key_local[:half]
    trail_ref[1] = key_local[half:]
    lead_ref[2] = value_local[:half]
    trail_ref[2] = value_local[half:]


def attend(query, key_rows, value, gradient, starts, same, first, heads, window, trailing):
    length = query.shape[0]
    columns = heads * HEAD_SIZE
    lead = length - trailing
    whole = pl.BlockSpec((length, HEAD_SIZE), lambda head, *_: (0, head + first))
    own = pl.BlockSpec((length, HEAD_SIZE), lambda head, *_: (0, head))
    return pl.pallas_call(
        functools.partial(attend_kernel, window),
        out_shape=(
            jax.ShapeDtypeStruct((3, lead, columns), jnp.bfloat16),
            jax.ShapeDtypeStruct((3, trailing, columns), jnp.bfloat16),
            jax.ShapeDtypeStruct((length, columns), jnp.bfloat16),
        ),
        grid_spec=pltpu.PrefetchScalarGridSpec(
            num_scalar_prefetch=2,
            grid=(heads,),
            in_specs=[whole, whole, whole, own],
            out_specs=(
                pl.BlockSpec((3, lead, HEAD_SIZE), lambda head, *_: (0, 0, head)),
                pl.BlockSpec((3, trailing, HEAD_SIZE), lambda head, *_: (0, 0, head)),
                own,
            ),
            scratch_shapes=[
                pltpu.VMEM((length, HEAD_SIZE), jnp.float32),
                pltpu.VMEM((length, HEAD_SIZE), jnp.float32),
            ],
        ),
        compiler_params=pltpu.CompilerParams(vmem_limit_bytes=32 * 1024 * 1024),
        cost_estimate=pl.CostEstimate(
            flops=10 * length * window * BLOCK * columns,
            bytes_accessed=16 * length * columns,
            transcendentals=length * window * BLOCK * heads,
        ),
    )(starts, same, query, key_rows, value, gradient)


def scattered(term, moved, tie):
    replicas = lax.axis_size("dp")
    position = lax.axis_index("dp")
    rows, columns = term.shape[0] // replicas, term.shape[1]
    remaining = list(reversed(range(replicas.bit_length() - 1)))
    for bit in range(replicas.bit_length() - 1):
        if bit == tie:
            term, moved = lax.optimization_barrier((term, moved))
        place = remaining.index(bit)
        remaining.pop(place)
        below = len(remaining) - place
        halves = term.reshape(1 << place, 2, (1 << below) * rows, columns)
        mine = (position >> bit) & 1
        sent = lax.dynamic_index_in_dim(halves, 1 - mine, 1, keepdims=False)
        kept = lax.dynamic_index_in_dim(halves, mine, 1, keepdims=False)
        arrived = lax.ppermute(sent, "dp", [(i, i ^ 1 << bit) for i in range(replicas)])
        total = kept.astype(jnp.float32) + arrived.astype(jnp.float32)
        term = total.reshape(-1, columns)
        if remaining:
            term = term.astype(jnp.bfloat16)
    return term, moved


def settle_kernel(blocks, moving, lead_ref, trail_ref, arrived_ref, *refs):
    outs = refs[-3:]
    half = lead_ref.shape[1]
    for which in range(3):
        outs[which][:half, :] = lead_ref[which]
        for block in range(trail_ref.shape[1] // BLOCK):
            rows = slice(block * BLOCK, (block + 1) * BLOCK)
            moved = half // BLOCK + block >= blocks - moving[0]

            @pl.when(moved)
            def _():
                outs[which][half + block * BLOCK : half + (block + 1) * BLOCK, :] = arrived_ref[which, rows]

            @pl.when(jnp.logical_not(moved))
            def _():
                outs[which][half + block * BLOCK : half + (block + 1) * BLOCK, :] = trail_ref[which, rows]


def settle(moving, lead, trail, arrived, first, heads, shape, earlier):
    step = lambda rows: pl.BlockSpec((3, rows, HEAD_SIZE), lambda head, *_: (0, 0, head))
    length = shape[0]
    return pl.pallas_call(
        functools.partial(settle_kernel, length // BLOCK),
        out_shape=(jax.ShapeDtypeStruct(shape, jnp.bfloat16),) * 3,
        grid_spec=pltpu.PrefetchScalarGridSpec(
            num_scalar_prefetch=1,
            grid=(heads,),
            in_specs=[step(lead.shape[1]), step(trail.shape[1]), step(trail.shape[1])]
            + [pl.BlockSpec(memory_space=pl.ANY)] * len(earlier),
            out_specs=(pl.BlockSpec((length, HEAD_SIZE), lambda head, *_: (0, head + first)),) * 3,
        ),
        input_output_aliases={4 + which: which for which in range(len(earlier))},
        compiler_params=pltpu.CompilerParams(vmem_limit_bytes=32 * 1024 * 1024),
        cost_estimate=pl.CostEstimate(
            flops=0, bytes_accessed=15 * length * heads * HEAD_SIZE, transcendentals=0
        ),
    )(moving.reshape(1), lead, trail, arrived, *earlier)


def shards(queries, keys, values, out_gradient, out_weight, segments, counts):
    full_gradient = lax.all_gather(out_gradient, "tensor", axis=0, tiled=True)
    replicas = lax.axis_size("dp")
    halfway = replicas // 2
    position = lax.axis_index("dp")
    blocks = segments.shape[1]
    window = blocks // 2
    trailing = window * BLOCK
    heads = queries.shape[1] // HEAD_SIZE
    groups = 2 if heads % 2 == 0 else min(heads, 3)
    each = heads // groups
    moving = lax.dynamic_index_in_dim(counts, position, 0, keepdims=False)
    ids = lax.dynamic_index_in_dim(segments, position, 0, keepdims=False)
    firsts = jnp.argmax(ids[:, None] == ids[None, :], axis=1).astype(jnp.int32)
    starts = jnp.minimum(firsts, blocks - window)
    near = jnp.take(ids, starts[:, None] + jnp.arange(window, dtype=jnp.int32)[None, :])
    same = (near == ids[:, None]).astype(jnp.int32).reshape(-1)
    pairs = [(i, (i + halfway) % replicas) for i in range(replicas)]

    moves, weight_parts = [], []
    for group in range(groups):
        width = each * HEAD_SIZE
        head_gradient = contract(
            full_gradient, out_weight[group * width : (group + 1) * width], ((1,), (1,))
        ).astype(jnp.bfloat16)
        lead, trail, head_output = attend(
            queries, keys, values, head_gradient, starts, same, group * each, each, window, trailing
        )
        if moves:
            head_output, moves[-1][2] = lax.optimization_barrier((head_output, moves[-1][2]))
        moves.append([lead, trail, lax.ppermute(trail, "dp", pairs)])
        term = (contract(full_gradient, head_output, ((0,), (0,))) / replicas).astype(jnp.bfloat16)
        part, moves[-1][2] = scattered(term, moves[-1][2], 2 if group == groups - 1 else None)
        weight_parts.append(part)

    settled = ()
    for group, (lead, trail, arrived) in enumerate(moves):
        settled = settle(
            moving, lead, trail, arrived, group * each, each, queries.shape, settled
        )
    return (*settled, jnp.concatenate(weight_parts, axis=1))


def solution(mesh):
    in_specs = (
        P("dp", "tensor"),
        P("dp", "tensor"),
        P("dp", "tensor"),
        P(("dp", "tensor"), None),
        P("tensor", None),
        P(),
        P(),
    )
    out_specs = (P("dp", "tensor"), P("dp", "tensor"), P("dp", "tensor"), P("dp", "tensor"))
    return jax.shard_map(shards, mesh=mesh, in_specs=in_specs, out_specs=out_specs, check_vma=False)
```
